32 devices in a mesh: narrow: 4 (over y, x), wide: 8 (over z, core).
Axes of the slice: x: 2, y: 2, z: 4, core: 2. Of those that a mesh axis runs over, the one named last changes fastest.
Arguments:
- slices: bfloat16 [32, 1024, 1024], P(None, 'narrow', 'wide'), may hold values from -6 to 6
- mode_one: bfloat16 [1024, 512], P('narrow', 'wide'), may hold values from -6 to 6
- mode_two: bfloat16 [1024, 512], P('wide', 'narrow'), may hold values from -6 to 6
- slice_table: bfloat16 [1024, 512], replicated, may hold values from 0.0099487305 to 0.079589844
- chosen: int32 [32], replicated, may hold values from 0 to 1023
Outputs:
- new_one: bfloat16 [1024, 512], P('narrow', 'wide')
- new_two: bfloat16 [1024, 512], P('wide', 'narrow')
The draws below stay inside these ranges and needn't reach their ends.
All inputs are finite; a program needn't handle non-finite values.
Results may differ from the reference program's by a relative error of at most 0.006.
Values may be sent and summed in bfloat16 or wider, within the bound.
A program may use at most 64 MiB of HBM per device.

```python
import math
import jax
import jax.numpy as jnp
from jax import lax

R = 512
BATCH = 32
KFULL = 1024
I = 1024
J = 1024


def plant(array, own_key, low, high):
    spot = [jax.random.randint(jax.random.fold_in(own_key, axis), (), 0, length) for axis, length in enumerate(array.shape)]
    main_axis = array.shape.index(max(array.shape))
    beside = spot[:main_axis] + [(spot[main_axis] + 1) % array.shape[main_axis]] + spot[main_axis + 1:]
    return array.at[tuple(spot)].set(low).at[tuple(beside)].set(high)


def level_of(key, shape, cuts, low, top_value):
    def one(dim, parts):
        heights = jax.random.uniform(jax.random.fold_in(jax.random.fold_in(key, 6), dim), (parts,), jnp.float32, low / len(cuts), top_value / len(cuts))
        return jnp.repeat(jnp.exp(heights), shape[dim] // parts).reshape((-1,) + (1,) * (len(shape) - dim - 1))

    level = one(*cuts[0])
    for cut in cuts[1:]:
        level = level * one(*cut)
    return level


def normal_values(stream_key, shape, spread, most, pieces=(), held_as=jnp.bfloat16):
    loudness = level_of(stream_key, shape, pieces, -0.22, 0.18) if pieces else 1.0
    drawn = jax.random.normal(stream_key, shape, jnp.float32) * spread * loudness
    return jnp.minimum(jnp.maximum(drawn, -most), most).astype(held_as)


def setup_inputs(seed: int = 0) -> dict:
    arg_keys = jax.random.split(jax.random.key(seed), 6)
    return {
        "slices": normal_values(arg_keys[0], (BATCH, I, J), 1.0, 6.0, ((1, 4), (2, 8))),
        "mode_one": normal_values(arg_keys[1], (I, R), 1.0, 6.0, ((0, 4), (1, 8))),
        "mode_two": normal_values(arg_keys[2], (J, R), 1.0, 6.0, ((0, 8), (1, 4))),
        "slice_table": jnp.clip(jnp.exp(jax.random.uniform(arg_keys[3], (KFULL, R), jnp.float32, math.log(0.0099487305), math.log(0.079589844))), 0.0099487305, 0.079589844).astype(jnp.bfloat16),
        "chosen": plant(jax.random.randint(arg_keys[4], (BATCH,), 0, KFULL), jax.random.fold_in(arg_keys[4], 1), 0, KFULL - 1).astype(jnp.int32),
    }


epsilon = 1e-06
step_size = 0.5

def renew(factor, gradient):
    inverse = lax.rsqrt(lax.optimization_barrier(jnp.mean(gradient * gradient, axis=1, keepdims=True)) + epsilon)
    return (factor.astype(jnp.float32) - step_size * gradient * inverse).astype(jnp.bfloat16)

def reference(slices, mode_one, mode_two, slice_table, chosen):
    slice_rows = jnp.take(slice_table, chosen.astype(jnp.int32), axis=0)
    second = mode_two.astype(jnp.float32)

    def sweep_one(total, inputs):
        target, row_scale = inputs
        scaled_two = (second * row_scale.astype(jnp.float32)[None, :]).astype(jnp.bfloat16)
        model_one = jnp.dot(mode_one, scaled_two.T, preferred_element_type=jnp.float32)
        error_one = jnp.tanh(model_one - target.astype(jnp.float32)).astype(jnp.bfloat16)
        return (total + jnp.dot(error_one, scaled_two, preferred_element_type=jnp.float32), None)
    grad_one, _ = lax.scan(sweep_one, jnp.zeros((I, R), jnp.float32), (slices, slice_rows))
    new_one = renew(mode_one, grad_one)
    first = new_one.astype(jnp.float32)

    def sweep_two(total, inputs):
        target, row_scale = inputs
        scaled_one = (first * row_scale.astype(jnp.float32)[None, :]).astype(jnp.bfloat16)
        model_two = jnp.dot(scaled_one, mode_two.T, preferred_element_type=jnp.float32)
        error_two = jnp.tanh(model_two - target.astype(jnp.float32)).astype(jnp.bfloat16)
        return (total + jnp.dot(error_two.T, scaled_one, preferred_element_type=jnp.float32), None)
    grad_two, _ = lax.scan(sweep_two, jnp.zeros((J, R), jnp.float32), (slices, slice_rows))
    new_two = renew(mode_two, grad_two)
    return (new_one, new_two)
```

```python
import functools
import jax
import jax.numpy as jnp
from jax import lax
from jax.experimental import pallas as pl
from jax.experimental.pallas import tpu as pltpu
from jax.sharding import PartitionSpec as P

epsilon = 1e-06
step_size = 0.5
f32 = jnp.float32
bf16 = jnp.bfloat16


def dot(a, b, dims):
    return lax.dot_general(a, b, (dims, ((), ())), preferred_element_type=f32)


def kernel(
    N, W, flip, step,
    slices_hbm, one_ref, two_ref, table_hbm, chosen_ref,
    out_one, out_two,
    slices, table, rows_s, one_t, two_blk, one_rows, two_rows, S, slices_t,
    grad, sib_in, rs_out, rs_in, new_rows, new_t, grad2, rs2_out, rs2_in, piece, piece_in,
    local_sem, gs, gr, fs, fr, ts, tr, ss, sr, rs, rr, ns, nr, ms, mr, us, ur, ps, pr,
):
    G = W // 2
    w = lax.axis_index("wide")
    n = lax.axis_index("narrow")
    g, c = w // 2, w % 2
    sib = {"wide": g * 2 + (1 - c)}
    K, I, J = slices.shape
    R = S.shape[1]

    def far(d):
        return {"wide": lax.rem(g + d, G) * 2 + c}

    def across(d):
        return {"narrow": lax.rem(n + d, N)}

    def send(src, dst, s, r, dev):
        copy = pltpu.make_async_remote_copy(
            src_ref=src, dst_ref=dst, send_sem=s, recv_sem=r,
            device_id=dev, device_id_type=pl.DeviceIdType.MESH,
        )
        copy.start()
        return copy

    load_table = pltpu.make_async_copy(table_hbm, table, local_sem.at[0])
    load_table.start()
    load_slices = pltpu.make_async_copy(slices_hbm, slices, local_sem.at[1])
    load_slices.start()

    barrier = pltpu.get_barrier_semaphore()
    partners = [sib] + [far(d) for d in range(1, G)] + [across(d) for d in range(1, N)]
    for dev in partners:
        pl.semaphore_signal(barrier, inc=1, device_id=dev, device_id_type=pl.DeviceIdType.MESH)
    pl.semaphore_wait(barrier, len(partners))

    sent = []

    def spread(own, buf, far_s, far_r, sib_s, sib_r):
        z = [send(own, buf.at[w], far_s.at[d], far_r.at[d], far(d)) for d in range(1, G)]
        f = [send(own, buf.at[w], sib_s.at[0], sib_r.at[0], sib)]

        def finish():
            for d in range(1, G):
                z[d - 1].wait_recv()
                at = buf.at[lax.rem(g - d + G, G) * 2 + c]
                f.append(send(at, at, sib_s.at[d], sib_r.at[d], sib))
            for copy in f:
                copy.wait_recv()
            sent.extend(z)
            sent.extend(f)

        return finish

    two_copies = [
        send(two_ref, two_blk.at[n], ts.at[d], tr.at[d], across(d)) for d in range(1, N)
    ]
    finish_one = spread(one_ref, one_t, gs, gr, fs, fr)
    two_blk[n] = two_ref[...]
    one_t[w] = one_ref[...]

    load_table.wait()
    hot = (
        lax.broadcasted_iota(jnp.int32, (table.shape[0], K), 0) == chosen_ref[...]
    ).astype(f32).astype(bf16)
    rows_s[...] = dot(hot, table[...], ((0,), (0,)))

    for copy in two_copies:
        copy.wait_recv()
    sent.extend(two_copies)
    if flip:
        two = two_blk[...].reshape(R, J).T
    else:
        two = jnp.concatenate([two_blk[m] for m in range(N)], axis=1)
    two_rows[...] = two.reshape(two_rows.shape)

    @pl.loop(0, K)
    def _(k):
        wide_two = two_rows[...].reshape(J, R).astype(f32)
        S[pl.ds(pl.multiple_of(k * J, J), J), :] = (wide_two * rows_s[pl.ds(k, 1), :]).astype(bf16)

    finish_one()
    one_rows[...] = one_t[...].reshape(R, I).T.reshape(one_rows.shape)
    load_slices.wait()
    grad[...] = jnp.zeros_like(grad)

    @pl.loop(0, K // step)
    def _(q):
        part = S[pl.ds(pl.multiple_of(q * step * J, step * J), step * J), :]
        model = dot(one_rows[...].reshape(I, R), part, ((1,), (1,)))
        target = jnp.concatenate([slices[q * step + m] for m in range(step)], axis=1)
        error = jnp.tanh(model - target.astype(f32)).astype(bf16)
        grad[...] += dot(error, part, ((1,), (0,))).reshape(grad.shape)

    halves = []
    for d in range(G):
        to = lax.rem(g + d + 1, G)
        halves.append(send(grad.at[to, 1 - c], sib_in.at[to], ss.at[d], sr.at[d], sib))
    shares = []
    for d in range(G):
        to = lax.rem(g + d + 1, G)
        halves[d].wait_recv()
        if d < G - 1:
            rs_out[to] = (grad[to, c] + sib_in[to]).astype(bf16)
            shares.append(send(rs_out.at[to], rs_in.at[g], rs.at[d], rr.at[d], far(d + 1)))
    total = grad[g, c] + sib_in[g]
    sent.extend(halves)

    @pl.loop(0, K)
    def _(k):
        slices_t[pl.ds(pl.multiple_of(k * J, J), J), :] = slices[k].T

    for d in range(G - 1):
        shares[d].wait_recv()
        total = total + rs_in[lax.rem(g - d - 1 + G, G)].astype(f32)
    sent.extend(shares)
    inverse = lax.rsqrt(jnp.sum(total * total, axis=1, keepdims=True) / R + epsilon)
    new_rows[w] = (one_rows[w].astype(f32) - step_size * total * inverse).astype(bf16)
    finish_new = spread(new_rows.at[w], new_rows, ns, nr, ms, mr)
    finish_new()
    new_t[...] = new_rows[...].reshape(I, R).T.reshape(new_t.shape)
    grad2[...] = jnp.zeros_like(grad2)

    @pl.loop(0, K // step)
    def _(q):
        at = pl.ds(pl.multiple_of(q * step * J, step * J), step * J)
        model = dot(S[at, :], new_t[...].reshape(R, I), ((1,), (0,)))
        error = jnp.tanh(model - slices_t[at, :].astype(f32)).astype(bf16)
        back = dot(error, new_rows[...].reshape(I, R), ((1,), (0,)))
        part = back[:J] * rows_s[pl.ds(q * step, 1), :]
        for m in range(1, step):
            part = part + back[m * J : (m + 1) * J] * rows_s[pl.ds(q * step + m, 1), :]
        grad2[...] += part.reshape(grad2.shape)

    rs2_out[...] = grad2[...].astype(bf16)
    shares2 = [
        send(rs2_out.at[lax.rem(n + d, N)], rs2_in.at[n], us.at[d], ur.at[d], across(d))
        for d in range(1, N)
    ]
    out_one[...] = new_t[w]
    total2 = grad2[n]
    for d in range(1, N):
        shares2[d - 1].wait_recv()
        total2 = total2 + rs2_in[lax.rem(n - d + N, N)].astype(f32)
    sent.extend(shares2)
    inverse2 = lax.rsqrt(jnp.sum(total2 * total2, axis=1, keepdims=True) / R + epsilon)
    fresh = (two_rows[n].astype(f32) - step_size * total2 * inverse2).astype(bf16)
    cols = R // N
    for m in range(N):
        piece[m] = fresh[:, m * cols : (m + 1) * cols]
    pieces = [
        send(piece.at[lax.rem(n + d, N)], piece_in.at[n], ps.at[d], pr.at[d], across(d))
        for d in range(1, N)
    ]
    piece_in[n] = piece[n]
    for copy in pieces:
        copy.wait_recv()
    out_two[...] = piece_in[...]
    sent.extend(pieces)
    for copy in sent:
        copy.wait_send()


def solution(mesh):
    N, W = mesh.shape["narrow"], mesh.shape["wide"]
    G = W // 2

    def body(slices, mode_one, mode_two, slice_table, chosen):
        K, I, J = slices.shape
        c1, c2 = mode_one.shape[1], mode_two.shape[1]
        R = c1 * W
        flip = c2 % 128 != 0
        step = next(s for s in (4, 2, 1) if K % s == 0)
        io, jo = I // W, J // N
        vm = pltpu.VMEM
        dma = pltpu.SemaphoreType.DMA
        in_vmem = pl.BlockSpec(memory_space=pltpu.VMEM)
        in_any = pl.BlockSpec(memory_space=pl.ANY)
        two = mode_two.T if flip else mode_two
        flops = 8 * K * I * J * R
        new_one, new_two = pl.pallas_call(
            functools.partial(kernel, N, W, flip, step),
            out_shape=(
                jax.ShapeDtypeStruct((c1, I), bf16),
                jax.ShapeDtypeStruct((N, jo, c2), bf16),
            ),
            in_specs=[in_any, in_vmem, in_vmem, in_any, in_vmem],
            out_specs=(in_vmem, in_vmem),
            scratch_shapes=[
                vm((K, I, J), bf16),
                vm(slice_table.shape, bf16),
                vm((K, R), f32),
                vm((W, c1, I), bf16),
                vm((N,) + two.shape, bf16),
                vm((W, io, R), bf16),
                vm((N, jo, R), bf16),
                vm((K * J, R), bf16),
                vm((K * J, I), bf16),
                vm((G, 2, io, R), f32),
                vm((G, io, R), f32),
                vm((G, io, R), bf16),
                vm((G, io, R), bf16),
                vm((W, io, R), bf16),
                vm((W, c1, I), bf16),
                vm((N, jo, R), f32),
                vm((N, jo, R), bf16),
                vm((N, jo, R), bf16),
                vm((N, jo, c2), bf16),
                vm((N, jo, c2), bf16),
                dma((2,)),
                dma((G,)), dma((G,)), dma((G,)), dma((G,)),
                dma((N,)), dma((N,)),
                dma((G,)), dma((G,)), dma((G,)), dma((G,)),
                dma((G,)), dma((G,)), dma((G,)), dma((G,)),
                dma((N,)), dma((N,)), dma((N,)), dma((N,)),
            ],
            compiler_params=pltpu.CompilerParams(
                collective_id=0, has_side_effects=True, vmem_limit_bytes=48 * 1024 * 1024
            ),
            cost_estimate=pl.CostEstimate(
                flops=flops, bytes_accessed=K * I * J * 2, transcendentals=2 * K * I * J
            ),
        )(slices, mode_one.T, two, slice_table, chosen.reshape(1, K))
        return new_one.T, new_two.reshape(J, c2)

    in_specs = (P(None, "narrow", "wide"), P("narrow", "wide"), P("wide", "narrow"), P(), P())
    out_specs = (P("narrow", "wide"), P("wide", "narrow"))
    return jax.shard_map(body, mesh=mesh, in_specs=in_specs, out_specs=out_specs, check_vma=False)
```

```python
import functools
import jax
import jax.numpy as jnp
from jax import lax
from jax.experimental import pallas as pl
from jax.experimental.pallas import tpu as pltpu
from jax.sharding import PartitionSpec as P

epsilon = 1e-06
step_size = 0.5
f32 = jnp.float32
bf16 = jnp.bfloat16


def dot(a, b, dims):
    return lax.dot_general(a, b, (dims, ((), ())), preferred_element_type=f32)


def kernel(
    N, W, flip, step,
    slices_hbm, one_hbm, two_hbm, table_hbm, chosen_hbm,
    one_out, two_out,
    slices, table, chosen, rows_s, one_t, two_blk, one_rows, two_rows, S, slices_t,
    grad, sib_in, rs_out, rs_in, new_rows, new_t, grad2, rs2_out, rs2_in, piece, piece_in,
    local_sem, gs, gr, fs, fr, ts, tr, ss, sr, rs, rr, ns, nr, ms, mr, us, ur, ps, pr,
):
    G = W // 2
    w = lax.axis_index("wide")
    n = lax.axis_index("narrow")
    g, c = w // 2, w % 2
    sib = {"wide": g * 2 + (1 - c)}
    K, I, J = slices.shape
    R = S.shape[1]

    def far(d):
        return {"wide": lax.rem(g + d, G) * 2 + c}

    def across(d):
        return {"narrow": lax.rem(n + d, N)}

    def send(src, dst, s, r, dev):
        copy = pltpu.make_async_remote_copy(
            src_ref=src, dst_ref=dst, send_sem=s, recv_sem=r,
            device_id=dev, device_id_type=pl.DeviceIdType.MESH,
        )
        copy.start()
        return copy

    load_table = pltpu.make_async_copy(table_hbm, table, local_sem.at[0])
    load_table.start()
    load_chosen = pltpu.make_async_copy(chosen_hbm, chosen, local_sem.at[2])
    load_chosen.start()
    load_two = pltpu.make_async_copy(two_hbm, two_blk.at[n], local_sem.at[3])
    load_two.start()
    load_one = pltpu.make_async_copy(one_hbm, one_t.at[w], local_sem.at[4])
    load_one.start()
    load_slices = pltpu.make_async_copy(slices_hbm, slices, local_sem.at[1])
    load_slices.start()

    barrier = pltpu.get_barrier_semaphore()
    partners = [sib] + [far(d) for d in range(1, G)] + [across(d) for d in range(1, N)]
    for dev in partners:
        pl.semaphore_signal(barrier, inc=1, device_id=dev, device_id_type=pl.DeviceIdType.MESH)
    load_table.wait()
    load_chosen.wait()
    hot = (
        lax.broadcasted_iota(jnp.int32, (table.shape[0], K), 0) == chosen[...]
    ).astype(f32).astype(bf16)
    rows_s[...] = dot(hot, table[...], ((0,), (0,)))
    load_slices.wait()

    @pl.loop(0, K)
    def _(k):
        slices_t[pl.ds(pl.multiple_of(k * J, J), J), :] = slices[k].T

    pl.semaphore_wait(barrier, len(partners))

    sent = []

    def sweep():
        while sent:
            sent.pop().wait_send()

    def spread(own, buf, far_s, far_r, sib_s, sib_r):
        z = [send(own, buf.at[w], far_s.at[d], far_r.at[d], far(d)) for d in range(1, G)]
        f = [send(own, buf.at[w], sib_s.at[0], sib_r.at[0], sib)]

        def finish():
            for d in range(1, G):
                z[d - 1].wait_recv()
                at = buf.at[lax.rem(g - d + G, G) * 2 + c]
                f.append(send(at, at, sib_s.at[d], sib_r.at[d], sib))
            for copy in f:
                copy.wait_recv()
            sent.extend(z)
            sent.extend(f)

        return finish

    two_copies = [
        send(two_hbm, two_blk.at[n], ts.at[d], tr.at[d], across(d)) for d in range(1, N)
    ]
    finish_one = spread(one_hbm, one_t, gs, gr, fs, fr)

    load_two.wait()
    for copy in two_copies:
        copy.wait_recv()
    sent.extend(two_copies)
    if flip:
        two = two_blk[...].reshape(R, J).T
    else:
        two = jnp.concatenate([two_blk[m] for m in range(N)], axis=1)
    two_rows[...] = two.reshape(two_rows.shape)

    @pl.loop(0, K)
    def _(k):
        wide_two = two_rows[...].reshape(J, R).astype(f32)
        S[pl.ds(pl.multiple_of(k * J, J), J), :] = (wide_two * rows_s[pl.ds(k, 1), :]).astype(bf16)

    load_one.wait()
    finish_one()
    one_rows[...] = one_t[...].reshape(R, I).T.reshape(one_rows.shape)
    grad[...] = jnp.zeros_like(grad)

    @pl.loop(0, K // step, unroll=4)
    def _(q):
        part = S[pl.ds(pl.multiple_of(q * step * J, step * J), step * J), :]
        model = dot(one_rows[...].reshape(I, R), part, ((1,), (1,)))
        target = jnp.concatenate([slices[q * step + m] for m in range(step)], axis=1)
        error = jnp.tanh(model - target.astype(f32)).astype(bf16)
        grad[...] += dot(error, part, ((1,), (0,))).reshape(grad.shape)

    sweep()
    halves = []
    for d in range(G):
        to = lax.rem(g + d + 1, G)
        halves.append(send(grad.at[to, 1 - c], sib_in.at[to], ss.at[d], sr.at[d], sib))
    shares = []
    for d in range(G):
        to = lax.rem(g + d + 1, G)
        halves[d].wait_recv()
        if d < G - 1:
            rs_out[to] = (grad[to, c] + sib_in[to]).astype(bf16)
            shares.append(send(rs_out.at[to], rs_in.at[g], rs.at[d], rr.at[d], far(d + 1)))
    total = grad[g, c] + sib_in[g]
    sent.extend(halves)

    sweep()
    for d in range(G - 1):
        shares[d].wait_recv()
        total = total + rs_in[lax.rem(g - d - 1 + G, G)].astype(f32)
    sent.extend(shares)
    inverse = lax.rsqrt(jnp.sum(total * total, axis=1, keepdims=True) / R + epsilon)
    new_rows[w] = (one_rows[w].astype(f32) - step_size * total * inverse).astype(bf16)
    finish_new = spread(new_rows.at[w], new_rows, ns, nr, ms, mr)
    finish_new()
    new_t[...] = new_rows[...].reshape(I, R).T.reshape(new_t.shape)
    grad2[...] = jnp.zeros_like(grad2)

    @pl.loop(0, K // step, unroll=4)
    def _(q):
        at = pl.ds(pl.multiple_of(q * step * J, step * J), step * J)
        model = dot(S[at, :], new_t[...].reshape(R, I), ((1,), (0,)))
        error = jnp.tanh(model - slices_t[at, :].astype(f32)).astype(bf16)
        back = dot(error, new_rows[...].reshape(I, R), ((1,), (0,)))
        part = back[:J] * rows_s[pl.ds(q * step, 1), :]
        for m in range(1, step):
            part = part + back[m * J : (m + 1) * J] * rows_s[pl.ds(q * step + m, 1), :]
        grad2[...] += part.reshape(grad2.shape)

    rs2_out[...] = grad2[...].astype(bf16)
    shares2 = [
        send(rs2_out.at[lax.rem(n + d, N)], rs2_in.at[n], us.at[d], ur.at[d], across(d))
        for d in range(1, N)
    ]
    one_out[...] = new_t[w]
    sweep()
    total2 = grad2[n]
    for d in range(1, N):
        shares2[d - 1].wait_recv()
        total2 = total2 + rs2_in[lax.rem(n - d + N, N)].astype(f32)
    sent.extend(shares2)
    inverse2 = lax.rsqrt(jnp.sum(total2 * total2, axis=1, keepdims=True) / R + epsilon)
    fresh = (two_rows[n].astype(f32) - step_size * total2 * inverse2).astype(bf16)
    cols = R // N
    for m in range(N):
        piece[m] = fresh[:, m * cols : (m + 1) * cols]
    pieces = [
        send(piece.at[lax.rem(n + d, N)], piece_in.at[n], ps.at[d], pr.at[d], across(d))
        for d in range(1, N)
    ]
    piece_in[n] = piece[n]
    sweep()
    for copy in pieces:
        copy.wait_recv()
    two_out[...] = piece_in[...]
    sent.extend(pieces)
    sweep()


def solution(mesh):
    N, W = mesh.shape["narrow"], mesh.shape["wide"]
    G = W // 2

    def body(slices, mode_one, mode_two, slice_table, chosen):
        K, I, J = slices.shape
        c1, c2 = mode_one.shape[1], mode_two.shape[1]
        R = c1 * W
        flip = c2 % 128 != 0
        step = next(s for s in (8, 4, 2, 1) if K % s == 0)
        io, jo = I // W, J // N
        vm = pltpu.VMEM
        dma = pltpu.SemaphoreType.DMA
        in_hbm = pl.BlockSpec(memory_space=pltpu.HBM)
        two = mode_two.T if flip else mode_two
        flops = 8 * K * I * J * R
        new_one, new_two = pl.pallas_call(
            functools.partial(kernel, N, W, flip, step),
            out_shape=(
                jax.ShapeDtypeStruct((c1, I), bf16),
                jax.ShapeDtypeStruct((N, jo, c2), bf16),
            ),
            in_specs=[in_hbm] * 5,
            out_specs=(pl.BlockSpec(memory_space=pltpu.VMEM),) * 2,
            scratch_shapes=[
                vm((K, I, J), bf16),
                vm(slice_table.shape, bf16),
                vm((1, K), jnp.int32),
                vm((K, R), f32),
                vm((W, c1, I), bf16),
                vm((N,) + two.shape, bf16),
                vm((W, io, R), bf16),
                vm((N, jo, R), bf16),
                vm((K * J, R), bf16),
                vm((K * J, I), bf16),
                vm((G, 2, io, R), f32),
                vm((G, io, R), f32),
                vm((G, io, R), bf16),
                vm((G, io, R), bf16),
                vm((W, io, R), bf16),
                vm((W, c1, I), bf16),
                vm((N, jo, R), f32),
                vm((N, jo, R), bf16),
                vm((N, jo, R), bf16),
                vm((N, jo, c2), bf16),
                vm((N, jo, c2), bf16),
                dma((5,)),
                dma((G,)), dma((G,)), dma((G,)), dma((G,)),
                dma((N,)), dma((N,)),
                dma((G,)), dma((G,)), dma((G,)), dma((G,)),
                dma((G,)), dma((G,)), dma((G,)), dma((G,)),
                dma((N,)), dma((N,)), dma((N,)), dma((N,)),
            ],
            compiler_params=pltpu.CompilerParams(
                collective_id=0, has_side_effects=True, vmem_limit_bytes=60 * 1024 * 1024
            ),
            cost_estimate=pl.CostEstimate(
                flops=flops, bytes_accessed=K * I * J * 2, transcendentals=2 * K * I * J
            ),
        )(slices, mode_one.T, two, slice_table, chosen.reshape(1, K))
        return new_one.T, new_two.reshape(J, c2)

    in_specs = (P(None, "narrow", "wide"), P("narrow", "wide"), P("wide", "narrow"), P(), P())
    out_specs = (P("narrow", "wide"), P("wide", "narrow"))
    return jax.shard_map(body, mesh=mesh, in_specs=in_specs, out_specs=out_specs, check_vma=False)
```

```python
import functools
import jax
import jax.numpy as jnp
from jax import lax
from jax.experimental import pallas as pl
from jax.experimental.pallas import tpu as pltpu
from jax.sharding import PartitionSpec as P

epsilon = 1e-06
step_size = 0.5
f32 = jnp.float32
bf16 = jnp.bfloat16


def dot(a, b, dims):
    return lax.dot_general(a, b, (dims, ((), ())), preferred_element_type=f32)


def kernel(
    N, W, flip, step,
    slices_hbm, one_hbm, two_hbm, table_hbm, chosen_hbm,
    one_out, two_out,
    slices, table, chosen, rows_s, one_t, two_blk, one_rows, two_rows, S, slices_t,
    grad, sib_in, rs_out, rs_in, new_rows, new_t, grad2, rs2_out, rs2_in, piece, piece_in,
    local_sem, gs, gr, fs, fr, ts, tr, ss, sr, rs, rr, ns, nr, ms, mr, us, ur, ps, pr,
):
    G = W // 2
    w = lax.axis_index("wide")
    n = lax.axis_index("narrow")
    g, c = w // 2, w % 2
    sib = {"wide": g * 2 + (1 - c)}
    K, I, J = slices.shape
    R = S.shape[1]

    def far(d):
        return {"wide": lax.rem(g + d, G) * 2 + c}

    def across(d):
        return {"narrow": lax.rem(n + d, N)}

    def send(src, dst, s, r, dev):
        copy = pltpu.make_async_remote_copy(
            src_ref=src, dst_ref=dst, send_sem=s, recv_sem=r,
            device_id=dev, device_id_type=pl.DeviceIdType.MESH,
        )
        copy.start()
        return copy

    load_table = pltpu.make_async_copy(table_hbm, table, local_sem.at[0])
    load_table.start()
    load_chosen = pltpu.make_async_copy(chosen_hbm, chosen, local_sem.at[2])
    load_chosen.start()
    load_two = pltpu.make_async_copy(two_hbm, two_blk.at[n], local_sem.at[3])
    load_two.start()
    load_one = pltpu.make_async_copy(one_hbm, one_t.at[w], local_sem.at[4])
    load_one.start()
    load_slices = pltpu.make_async_copy(slices_hbm, slices, local_sem.at[1])
    load_slices.start()

    barrier = pltpu.get_barrier_semaphore()
    partners = [sib] + [far(d) for d in range(1, G)] + [across(d) for d in range(1, N)]
    for dev in partners:
        pl.semaphore_signal(barrier, inc=1, device_id=dev, device_id_type=pl.DeviceIdType.MESH)
    load_table.wait()
    load_chosen.wait()
    hot = (
        lax.broadcasted_iota(jnp.int32, (table.shape[0], K), 0) == chosen[...]
    ).astype(f32).astype(bf16)
    rows_s[...] = dot(hot, table[...], ((0,), (0,)))
    load_slices.wait()

    @pl.loop(0, K, unroll=4)
    def _(k):
        slices_t[pl.ds(pl.multiple_of(k * J, J), J), :] = slices[k].T

    pl.semaphore_wait(barrier, len(partners))

    sent = []

    def sweep():
        while sent:
            sent.pop().wait_send()

    def spread(own, buf, far_s, far_r, sib_s, sib_r):
        z = [send(own, buf.at[w], far_s.at[d], far_r.at[d], far(d)) for d in range(1, G)]
        f = [send(own, buf.at[w], sib_s.at[0], sib_r.at[0], sib)]

        def finish():
            for d in range(1, G):
                z[d - 1].wait_recv()
                at = buf.at[lax.rem(g - d + G, G) * 2 + c]
                f.append(send(at, at, sib_s.at[d], sib_r.at[d], sib))
            for copy in f:
                copy.wait_recv()
            sent.extend(z)
            sent.extend(f)

        return finish

    two_copies = [
        send(two_hbm, two_blk.at[n], ts.at[d], tr.at[d], across(d)) for d in range(1, N)
    ]
    finish_one = spread(one_hbm, one_t, gs, gr, fs, fr)

    load_two.wait()
    for copy in two_copies:
        copy.wait_recv()
    sent.extend(two_copies)
    if flip:
        two = two_blk[...].reshape(R, J).T
    else:
        two = jnp.concatenate([two_blk[m] for m in range(N)], axis=1)
    two_rows[...] = two.reshape(two_rows.shape)

    @pl.loop(0, K, unroll=4)
    def _(k):
        wide_two = two_rows[...].reshape(J, R).astype(f32)
        S[pl.ds(pl.multiple_of(k * J, J), J), :] = (wide_two * rows_s[pl.ds(k, 1), :]).astype(bf16)

    load_one.wait()
    finish_one()
    one_rows[...] = one_t[...].reshape(R, I).T.reshape(one_rows.shape)
    grad[...] = jnp.zeros_like(grad)

    @pl.loop(0, K // step, unroll=4)
    def _(q):
        part = S[pl.ds(pl.multiple_of(q * step * J, step * J), step * J), :]
        model = dot(one_rows[...].reshape(I, R), part, ((1,), (1,)))
        target = jnp.concatenate([slices[q * step + m] for m in range(step)], axis=1)
        error = jnp.tanh(model - target.astype(f32)).astype(bf16)
        grad[...] += dot(error, part, ((1,), (0,))).reshape(grad.shape)

    sweep()
    halves = []
    for d in range(G):
        to = lax.rem(g + d + 1, G)
        halves.append(send(grad.at[to, 1 - c], sib_in.at[to], ss.at[d], sr.at[d], sib))
    shares = []
    for d in range(G):
        to = lax.rem(g + d + 1, G)
        halves[d].wait_recv()
        if d < G - 1:
            rs_out[to] = (grad[to, c] + sib_in[to]).astype(bf16)
            shares.append(send(rs_out.at[to], rs_in.at[g], rs.at[d], rr.at[d], far(d + 1)))
    total = grad[g, c] + sib_in[g]
    sent.extend(halves)

    sweep()
    for d in range(G - 1):
        shares[d].wait_recv()
        total = total + rs_in[lax.rem(g - d - 1 + G, G)].astype(f32)
    sent.extend(shares)
    inverse = lax.rsqrt(jnp.sum(total * total, axis=1, keepdims=True) / R + epsilon)
    new_rows[w] = (one_rows[w].astype(f32) - step_size * total * inverse).astype(bf16)
    finish_new = spread(new_rows.at[w], new_rows, ns, nr, ms, mr)
    finish_new()
    new_t[...] = new_rows[...].reshape(I, R).T.reshape(new_t.shape)
    grad2[...] = jnp.zeros_like(grad2)

    @pl.loop(0, K // step, unroll=4)
    def _(q):
        at = pl.ds(pl.multiple_of(q * step * J, step * J), step * J)
        model = dot(S[at, :], new_t[...].reshape(R, I), ((1,), (0,)))
        error = jnp.tanh(model - slices_t[at, :].astype(f32)).astype(bf16)
        back = dot(error, new_rows[...].reshape(I, R), ((1,), (0,)))
        part = back[:J] * rows_s[pl.ds(q * step, 1), :]
        for m in range(1, step):
            part = part + back[m * J : (m + 1) * J] * rows_s[pl.ds(q * step + m, 1), :]
        grad2[...] += part.reshape(grad2.shape)

    rs2_out[...] = grad2[...].astype(bf16)
    shares2 = [
        send(rs2_out.at[lax.rem(n + d, N)], rs2_in.at[n], us.at[d], ur.at[d], across(d))
        for d in range(1, N)
    ]
    one_out[...] = new_t[w]
    sweep()
    total2 = grad2[n]
    for d in range(1, N):
        shares2[d - 1].wait_recv()
        total2 = total2 + rs2_in[lax.rem(n - d + N, N)].astype(f32)
    sent.extend(shares2)
    inverse2 = lax.rsqrt(jnp.sum(total2 * total2, axis=1, keepdims=True) / R + epsilon)
    fresh = (two_rows[n].astype(f32) - step_size * total2 * inverse2).astype(bf16)
    cols = R // N
    for m in range(N):
        piece[m] = fresh[:, m * cols : (m + 1) * cols]
    pieces = [
        send(piece.at[lax.rem(n + d, N)], piece_in.at[n], ps.at[d], pr.at[d], across(d))
        for d in range(1, N)
    ]
    piece_in[n] = piece[n]
    sweep()
    for copy in pieces:
        copy.wait_recv()
    two_out[...] = piece_in[...]
    sent.extend(pieces)
    sweep()


def settle(one_ref, two_ref, one_out, two_out, sem):
    first = pltpu.make_async_copy(one_ref, one_out, sem.at[0])
    second = pltpu.make_async_copy(two_ref, two_out, sem.at[1])
    first.start()
    second.start()
    first.wait()
    second.wait()


def solution(mesh):
    N, W = mesh.shape["narrow"], mesh.shape["wide"]
    G = W // 2

    def body(slices, mode_one, mode_two, slice_table, chosen):
        K, I, J = slices.shape
        c1, c2 = mode_one.shape[1], mode_two.shape[1]
        R = c1 * W
        flip = c2 % 128 != 0
        step = next(s for s in (8, 4, 2, 1) if K % s == 0)
        io, jo = I // W, J // N
        vm = pltpu.VMEM
        dma = pltpu.SemaphoreType.DMA
        in_hbm = pl.BlockSpec(memory_space=pltpu.HBM)
        two = mode_two.T if flip else mode_two
        flops = 8 * K * I * J * R
        new_one, new_two = pl.pallas_call(
            functools.partial(kernel, N, W, flip, step),
            out_shape=(
                jax.ShapeDtypeStruct((c1, I), bf16),
                jax.ShapeDtypeStruct((N, jo, c2), bf16),
            ),
            in_specs=[in_hbm] * 5,
            out_specs=(pl.BlockSpec(memory_space=pltpu.VMEM),) * 2,
            scratch_shapes=[
                vm((K, I, J), bf16),
                vm(slice_table.shape, bf16),
                vm((1, K), jnp.int32),
                vm((K, R), f32),
                vm((W, c1, I), bf16),
                vm((N,) + two.shape, bf16),
                vm((W, io, R), bf16),
                vm((N, jo, R), bf16),
                vm((K * J, R), bf16),
                vm((K * J, I), bf16),
                vm((G, 2, io, R), f32),
                vm((G, io, R), f32),
                vm((G, io, R), bf16),
                vm((G, io, R), bf16),
                vm((W, io, R), bf16),
                vm((W, c1, I), bf16),
                vm((N, jo, R), f32),
                vm((N, jo, R), bf16),
                vm((N, jo, R), bf16),
                vm((N, jo, c2), bf16),
                vm((N, jo, c2), bf16),
                dma((5,)),
                dma((G,)), dma((G,)), dma((G,)), dma((G,)),
                dma((N,)), dma((N,)),
                dma((G,)), dma((G,)), dma((G,)), dma((G,)),
                dma((G,)), dma((G,)), dma((G,)), dma((G,)),
                dma((N,)), dma((N,)), dma((N,)), dma((N,)),
            ],
            compiler_params=pltpu.CompilerParams(
                collective_id=0, has_side_effects=True, vmem_limit_bytes=60 * 1024 * 1024
            ),
            cost_estimate=pl.CostEstimate(
                flops=flops, bytes_accessed=K * I * J * 2, transcendentals=2 * K * I * J
            ),
        )(slices, mode_one.T, two, slice_table, chosen.reshape(1, K))
        vspec = pl.BlockSpec(memory_space=pltpu.VMEM)
        new_one, new_two = pl.pallas_call(
            settle,
            out_shape=(
                jax.ShapeDtypeStruct(new_one.shape, bf16),
                jax.ShapeDtypeStruct(new_two.shape, bf16),
            ),
            in_specs=[vspec] * 2,
            out_specs=(pl.BlockSpec(memory_space=pl.ANY),) * 2,
            scratch_shapes=[pltpu.SemaphoreType.DMA((2,))],
            compiler_params=pltpu.CompilerParams(vmem_limit_bytes=60 * 1024 * 1024),
        )(new_one, new_two)
        return new_one.T, new_two.reshape(J, c2)

    in_specs = (P(None, "narrow", "wide"), P("narrow", "wide"), P("wide", "narrow"), P(), P())
    out_specs = (P("narrow", "wide"), P("wide", "narrow"))
    return jax.shard_map(body, mesh=mesh, in_specs=in_specs, out_specs=out_specs, check_vma=False)
```

```python
import functools
import jax
import jax.numpy as jnp
from jax import lax
from jax.experimental import pallas as pl
from jax.experimental.pallas import tpu as pltpu
from jax.sharding import PartitionSpec as P

epsilon = 1e-06
step_size = 0.5
f32 = jnp.float32
bf16 = jnp.bfloat16


def dot(a, b, dims):
    return lax.dot_general(a, b, (dims, ((), ())), preferred_element_type=f32)


def kernel(
    N, W, flip, step,
    slices_hbm, one_hbm, two_hbm, table_hbm, chosen_hbm,
    one_out, two_out,
    slices, table, chosen, rows_s, one_t, two_blk, one_rows, two_rows, S, slices_t,
    grad, sib_in, rs_out, rs_in, new_rows, new_t, grad2, rs2_out, rs2_in, piece, piece_in,
    local_sem, gs, gr, fs, fr, ts, tr, ss, sr, rs, rr, ns, nr, ms, mr, us, ur, ps, pr,
):
    G = W // 2
    w = lax.axis_index("wide")
    n = lax.axis_index("narrow")
    g, c = w // 2, w % 2
    sib = {"wide": g * 2 + (1 - c)}
    K, I, J = slices.shape
    R = S.shape[1]

    def far(d):
        return {"wide": lax.rem(g + d, G) * 2 + c}

    def across(d):
        return {"narrow": lax.rem(n + d, N)}

    def send(src, dst, s, r, dev):
        copy = pltpu.make_async_remote_copy(
            src_ref=src, dst_ref=dst, send_sem=s, recv_sem=r,
            device_id=dev, device_id_type=pl.DeviceIdType.MESH,
        )
        copy.start()
        return copy

    load_table = pltpu.make_async_copy(table_hbm, table, local_sem.at[0])
    load_table.start()
    load_chosen = pltpu.make_async_copy(chosen_hbm, chosen, local_sem.at[2])
    load_chosen.start()
    load_two = pltpu.make_async_copy(two_hbm, two_blk.at[n], local_sem.at[3])
    load_two.start()
    load_one = pltpu.make_async_copy(one_hbm, one_t.at[w], local_sem.at[4])
    load_one.start()
    load_slices = pltpu.make_async_copy(slices_hbm, slices, local_sem.at[1])
    load_slices.start()

    barrier = pltpu.get_barrier_semaphore()
    partners = [sib] + [far(d) for d in range(1, G)] + [across(d) for d in range(1, N)]
    for dev in partners:
        pl.semaphore_signal(barrier, inc=1, device_id=dev, device_id_type=pl.DeviceIdType.MESH)
    load_table.wait()
    load_chosen.wait()
    hot = (
        lax.broadcasted_iota(jnp.int32, (table.shape[0], K), 0) == chosen[...]
    ).astype(f32).astype(bf16)
    rows_s[...] = dot(hot, table[...], ((0,), (0,)))
    load_slices.wait()

    @pl.loop(0, K, unroll=8)
    def _(k):
        slices_t[pl.ds(pl.multiple_of(k * J, J), J), :] = slices[k].T

    pl.semaphore_wait(barrier, len(partners))

    sent = []

    def sweep():
        while sent:
            sent.pop().wait_send()

    def spread(own, buf, far_s, far_r, sib_s, sib_r):
        z = [send(own, buf.at[w], far_s.at[d], far_r.at[d], far(d)) for d in range(1, G)]
        f = [send(own, buf.at[w], sib_s.at[0], sib_r.at[0], sib)]

        def finish():
            for d in range(1, G):
                z[d - 1].wait_recv()
                at = buf.at[lax.rem(g - d + G, G) * 2 + c]
                f.append(send(at, at, sib_s.at[d], sib_r.at[d], sib))
            for copy in f:
                copy.wait_recv()
            sent.extend(z)
            sent.extend(f)

        return finish

    two_copies = [
        send(two_hbm, two_blk.at[n], ts.at[d], tr.at[d], across(d)) for d in range(1, N)
    ]
    finish_one = spread(one_hbm, one_t, gs, gr, fs, fr)

    load_two.wait()
    for copy in two_copies:
        copy.wait_recv()
    sent.extend(two_copies)
    if flip:
        two = two_blk[...].reshape(R, J).T
    else:
        two = jnp.concatenate([two_blk[m] for m in range(N)], axis=1)
    two_rows[...] = two.reshape(two_rows.shape)

    @pl.loop(0, K, unroll=8)
    def _(k):
        wide_two = two_rows[...].reshape(J, R).astype(f32)
        S[pl.ds(pl.multiple_of(k * J, J), J), :] = (wide_two * rows_s[pl.ds(k, 1), :]).astype(bf16)

    load_one.wait()
    finish_one()
    one_rows[...] = one_t[...].reshape(R, I).T.reshape(one_rows.shape)
    grad[...] = jnp.zeros_like(grad)

    @pl.loop(0, K // step, unroll=4)
    def _(q):
        part = S[pl.ds(pl.multiple_of(q * step * J, step * J), step * J), :]
        model = dot(one_rows[...].reshape(I, R), part, ((1,), (1,)))
        target = jnp.concatenate([slices[q * step + m] for m in range(step)], axis=1)
        error = jnp.tanh(model - target.astype(f32)).astype(bf16)
        grad[...] += dot(error, part, ((1,), (0,))).reshape(grad.shape)

    sweep()
    halves = []
    for d in range(G):
        to = lax.rem(g + d + 1, G)
        halves.append(send(grad.at[to, 1 - c], sib_in.at[to], ss.at[d], sr.at[d], sib))
    shares = []
    for d in range(G):
        to = lax.rem(g + d + 1, G)
        halves[d].wait_recv()
        if d < G - 1:
            rs_out[to] = (grad[to, c] + sib_in[to]).astype(bf16)
            shares.append(send(rs_out.at[to], rs_in.at[g], rs.at[d], rr.at[d], far(d + 1)))
    total = grad[g, c] + sib_in[g]
    sent.extend(halves)

    sweep()
    for d in range(G - 1):
        shares[d].wait_recv()
        total = total + rs_in[lax.rem(g - d - 1 + G, G)].astype(f32)
    sent.extend(shares)
    inverse = lax.rsqrt(jnp.sum(total * total, axis=1, keepdims=True) / R + epsilon)
    new_rows[w] = (one_rows[w].astype(f32) - step_size * total * inverse).astype(bf16)
    finish_new = spread(new_rows.at[w], new_rows, ns, nr, ms, mr)
    finish_new()
    new_t[...] = new_rows[...].reshape(I, R).T.reshape(new_t.shape)
    grad2[...] = jnp.zeros_like(grad2)

    @pl.loop(0, K // step, unroll=4)
    def _(q):
        at = pl.ds(pl.multiple_of(q * step * J, step * J), step * J)
        model = dot(S[at, :], new_t[...].reshape(R, I), ((1,), (0,)))
        error = jnp.tanh(model - slices_t[at, :].astype(f32)).astype(bf16)
        back = dot(error, new_rows[...].reshape(I, R), ((1,), (0,)))
        part = back[:J] * rows_s[pl.ds(q * step, 1), :]
        for m in range(1, step):
            part = part + back[m * J : (m + 1) * J] * rows_s[pl.ds(q * step + m, 1), :]
        grad2[...] += part.reshape(grad2.shape)

    rs2_out[...] = grad2[...].astype(bf16)
    shares2 = [
        send(rs2_out.at[lax.rem(n + d, N)], rs2_in.at[n], us.at[d], ur.at[d], across(d))
        for d in range(1, N)
    ]
    one_out[...] = new_t[w]
    sweep()
    total2 = grad2[n]
    for d in range(1, N):
        shares2[d - 1].wait_recv()
        total2 = total2 + rs2_in[lax.rem(n - d + N, N)].astype(f32)
    sent.extend(shares2)
    inverse2 = lax.rsqrt(jnp.sum(total2 * total2, axis=1, keepdims=True) / R + epsilon)
    fresh = (two_rows[n].astype(f32) - step_size * total2 * inverse2).astype(bf16)
    cols = R // N
    for m in range(N):
        piece[m] = fresh[:, m * cols : (m + 1) * cols]
    pieces = [
        send(piece.at[lax.rem(n + d, N)], piece_in.at[n], ps.at[d], pr.at[d], across(d))
        for d in range(1, N)
    ]
    piece_in[n] = piece[n]
    sweep()
    for copy in pieces:
        copy.wait_recv()
    two_out[...] = piece_in[...]
    sent.extend(pieces)
    sweep()


def settle(one_ref, two_ref, one_out, two_out, sem):
    first = pltpu.make_async_copy(one_ref, one_out, sem.at[0])
    second = pltpu.make_async_copy(two_ref, two_out, sem.at[1])
    first.start()
    second.start()
    first.wait()
    second.wait()


def solution(mesh):
    N, W = mesh.shape["narrow"], mesh.shape["wide"]
    G = W // 2

    def body(slices, mode_one, mode_two, slice_table, chosen):
        K, I, J = slices.shape
        c1, c2 = mode_one.shape[1], mode_two.shape[1]
        R = c1 * W
        flip = c2 % 128 != 0
        step = next(s for s in (8, 4, 2, 1) if K % s == 0)
        io, jo = I // W, J // N
        vm = pltpu.VMEM
        dma = pltpu.SemaphoreType.DMA
        in_hbm = pl.BlockSpec(memory_space=pltpu.HBM)
        two = mode_two.T if flip else mode_two
        flops = 8 * K * I * J * R
        new_one, new_two = pl.pallas_call(
            functools.partial(kernel, N, W, flip, step),
            out_shape=(
                jax.ShapeDtypeStruct((c1, I), bf16),
                jax.ShapeDtypeStruct((N, jo, c2), bf16),
            ),
            in_specs=[in_hbm] * 5,
            out_specs=(pl.BlockSpec(memory_space=pltpu.VMEM),) * 2,
            scratch_shapes=[
                vm((K, I, J), bf16),
                vm(slice_table.shape, bf16),
                vm((1, K), jnp.int32),
                vm((K, R), f32),
                vm((W, c1, I), bf16),
                vm((N,) + two.shape, bf16),
                vm((W, io, R), bf16),
                vm((N, jo, R), bf16),
                vm((K * J, R), bf16),
                vm((K * J, I), bf16),
                vm((G, 2, io, R), f32),
                vm((G, io, R), f32),
                vm((G, io, R), bf16),
                vm((G, io, R), bf16),
                vm((W, io, R), bf16),
                vm((W, c1, I), bf16),
                vm((N, jo, R), f32),
                vm((N, jo, R), bf16),
                vm((N, jo, R), bf16),
                vm((N, jo, c2), bf16),
                vm((N, jo, c2), bf16),
                dma((5,)),
                dma((G,)), dma((G,)), dma((G,)), dma((G,)),
                dma((N,)), dma((N,)),
                dma((G,)), dma((G,)), dma((G,)), dma((G,)),
                dma((G,)), dma((G,)), dma((G,)), dma((G,)),
                dma((N,)), dma((N,)), dma((N,)), dma((N,)),
            ],
            compiler_params=pltpu.CompilerParams(
                collective_id=0, has_side_effects=True, vmem_limit_bytes=60 * 1024 * 1024
            ),
            cost_estimate=pl.CostEstimate(
                flops=flops, bytes_accessed=K * I * J * 2, transcendentals=2 * K * I * J
            ),
        )(slices, mode_one.T, two, slice_table, chosen.reshape(1, K))
        vspec = pl.BlockSpec(memory_space=pltpu.VMEM)
        new_one, new_two = pl.pallas_call(
            settle,
            out_shape=(
                jax.ShapeDtypeStruct(new_one.shape, bf16),
                jax.ShapeDtypeStruct(new_two.shape, bf16),
            ),
            in_specs=[vspec] * 2,
            out_specs=(pl.BlockSpec(memory_space=pl.ANY),) * 2,
            scratch_shapes=[pltpu.SemaphoreType.DMA((2,))],
            compiler_params=pltpu.CompilerParams(vmem_limit_bytes=60 * 1024 * 1024),
        )(new_one, new_two)
        return new_one.T, new_two.reshape(J, c2)

    in_specs = (P(None, "narrow", "wide"), P("narrow", "wide"), P("wide", "narrow"), P(), P())
    out_specs = (P("narrow", "wide"), P("wide", "narrow"))
    return jax.shard_map(body, mesh=mesh, in_specs=in_specs, out_specs=out_specs, check_vma=False)
```
